256 devices in a mesh: src: 16 (over y_lo, x, core), dst: 16 (over z, y_hi).
Axes of the slice: x: 4, y: 4 (y_hi: 2, y_lo: 2; y = y_hi * 2 + y_lo), z: 8, core: 2. Of those that a mesh axis runs over, the one named last changes fastest.
Arguments:
- plan: int32 [2, 2], replicated, may hold values from 1 to 15, as said below
- lhs_ids: int32 [2, 2048, 256], P(None, ('src', 'dst')), may hold values from 0 to 383
- rhs_ids: int32 [2, 2048, 256], P(None, ('src', 'dst')), may hold values from 0 to 383
- rel_ids: int32 [2, 2048, 256], P(None, ('src', 'dst')), may hold values from 0 to 63, as said below
- neg_ids: int32 [2, 2048, 256], P(None, ('src', 'dst')), may hold values from 0 to 383
- lengths: int32 [2, 2048], P(None, ('src', 'dst')), may hold values from 0 to 256, as said below
- lhs_emb: float32 [256, 384, 256], P(('src', 'dst')), may hold values from -1.5 to 1.5
- lhs_acc: float32 [256, 384], P(('src', 'dst')), may hold values from 0.01 to 1
- rhs_emb: float32 [256, 384, 256], P(('src', 'dst')), may hold values from -1.5 to 1.5
- rhs_acc: float32 [256, 384], P(('src', 'dst')), may hold values from 0.01 to 1
- relation: float32 [64, 256], replicated, may hold values from 0.1 to 1.9
- rel_acc: float32 [64], replicated, may hold values from 0.01 to 1
Outputs:
- lhs_out: float32 [256, 384, 256], P(('src', 'dst'))
- lhs_acc_out: float32 [256, 384], P(('src', 'dst'))
- rhs_out: float32 [256, 384, 256], P(('src', 'dst'))
- rhs_acc_out: float32 [256, 384], P(('src', 'dst'))
- relation_out: float32 [64, 256], replicated
- rel_acc_out: float32 [64], replicated
The draws below stay inside these ranges and needn't reach their ends.
Inputs may be any that keep to these rules, and one draw needn't show every extreme that they name: `plan`: row r holds round r's offsets, column 0 along src and column 1 along dst, each below that axis's size; in each column an offset differs from the previous round's, and some round has 15 in column 0 and some round 16 - 1 in column 1. `lengths`: within one bucket's 8 batches of one round, every batch before the last nonzero one is full and every batch after it is 0; in every round some bucket has all its batches full. `rel_ids`: the relation types of one bucket's edge slots in one round lie within 4 consecutive type numbers, counted modulo 64.
All inputs are finite; a program needn't handle non-finite values.
Results may differ from the reference program's by a relative error of at most 0.0003.
Values sent between devices are 32-bit elements; how exact they have to be, the bound alone decides.
No kernel may reach another device: no remote copies, remote signals or barrier semaphores. Data moves between devices by JAX's collectives and lax.ppermute only.
A program may use at most 64 MiB of HBM per device.

```python
import math
import jax
import jax.numpy as jnp
from jax import lax

D = 256
NREL = 64
ROWS = 384
BATCHES = 8
BATCH = 256
NNEG = 256
ROUNDS = 2
NPART = 256
N_SRC = 16
N_DST = 16


def offset_column(subkey, extent):
    full_round = jax.random.randint(jax.random.fold_in(subkey, 100), (), 0, ROUNDS)
    previous = jnp.int32(0)
    entries = []
    for round_no in range(ROUNDS):
        round_key = jax.random.fold_in(subkey, round_no)
        narrow = jax.random.randint(round_key, (), 1, extent - 2)
        narrow = narrow + (narrow >= previous).astype(jnp.int32)
        loose = jax.random.randint(jax.random.fold_in(round_key, 7), (), 1, extent - 1)
        picked = jnp.where((previous == extent - 1) | (previous == 0), loose, narrow)
        picked = jnp.where(round_no == full_round, extent - 1, picked)
        entries.append(picked)
        previous = picked
    return jnp.stack(entries)


def draw_plan(key, part):
    key = jax.random.fold_in(key, 11)
    first_column = offset_column(jax.random.fold_in(key, 1), N_SRC)
    second_column = offset_column(jax.random.fold_in(key, 2), N_DST)
    return jnp.stack([first_column, second_column], axis=1).astype(jnp.int32)


def draw_rel_ids(key, part):
    key = jax.random.fold_in(key, 23)
    first_type = jax.random.randint(jax.random.fold_in(key, 1), (ROUNDS, NPART, 1, 1), 0, NREL)
    spread_type = jax.random.randint(jax.random.fold_in(key, 2), (ROUNDS, NPART, BATCHES, BATCH), 0, 4)
    return ((first_type + spread_type) % NREL).reshape(ROUNDS, NPART * BATCHES, BATCH).astype(jnp.int32)


def draw_lengths(key, part):
    key = jax.random.fold_in(key, 37)
    heavy = jax.random.randint(jax.random.fold_in(key, 1), (ROUNDS, NPART), 0, 4) == 3
    forced = jax.random.randint(jax.random.fold_in(key, 2), (ROUNDS, 1), 0, NPART)
    device_no = jnp.arange(NPART, dtype=jnp.int32)[None, :]
    is_forced = device_no == forced
    weight = jnp.where(heavy | is_forced, 4, 1)
    shortfall = jax.random.randint(jax.random.fold_in(key, 3), (ROUNDS, NPART), 0, BATCH // 2)
    shortfall = jnp.where(is_forced, 0, shortfall)
    total = weight * BATCHES * BATCH // 4 - shortfall
    batch_no = jnp.arange(BATCHES, dtype=jnp.int32)
    filled = jnp.clip(total[:, :, None] - batch_no[None, None, :] * BATCH, 0, BATCH)
    return filled.reshape(ROUNDS, NPART * BATCHES).astype(jnp.int32)


def set_ends(values, own_key, low, high):
    longest = values.shape.index(max(values.shape))
    spots = []
    for shift in (0, 1):
        where = [jax.random.randint(jax.random.fold_in(own_key, axis), (), 0, length) for axis, length in enumerate(values.shape)]
        where[longest] = (where[longest] + shift) % values.shape[longest]
        spots.append(tuple(where))
    return values.at[spots[0]].set(low).at[spots[1]].set(high)


def block_scale(key, dims, pieces, least, largest):
    loudness, own = 1.0, jax.random.fold_in(key, 6)
    for dim, parts in pieces:
        steps = jnp.exp(jax.random.uniform(jax.random.fold_in(own, dim), (parts,), jnp.float32, least / len(pieces), largest / len(pieces)))
        loudness = loudness * jnp.repeat(steps, dims[dim] // parts).reshape([-1 if axis == dim else 1 for axis in range(len(dims))])
    return loudness


def bell_draw(stream_key, shape, width, limit, cuts=(), kind=jnp.bfloat16):
    values = width * jax.random.normal(stream_key, shape, jnp.float32)
    if cuts:
        values = values * block_scale(stream_key, shape, cuts, -0.22, 0.18)
    return jnp.clip(values, -limit, limit).astype(kind)


def setup_inputs(seed: int = 0) -> dict:
    key_list = jax.random.split(jax.random.key(seed), 13)
    return {
        "plan": draw_plan(jax.random.fold_in(key_list[12], 71), 0),
        "lhs_ids": set_ends(jax.random.randint(key_list[1], (ROUNDS, NPART * BATCHES, BATCH), 0, ROWS), jax.random.fold_in(key_list[1], 1), 0, ROWS - 1).astype(jnp.int32),
        "rhs_ids": set_ends(jax.random.randint(key_list[2], (ROUNDS, NPART * BATCHES, BATCH), 0, ROWS), jax.random.fold_in(key_list[2], 1), 0, ROWS - 1).astype(jnp.int32),
        "rel_ids": draw_rel_ids(jax.random.fold_in(key_list[12], 71), 0),
        "neg_ids": set_ends(jax.random.randint(key_list[4], (ROUNDS, NPART * BATCHES, NNEG), 0, ROWS), jax.random.fold_in(key_list[4], 1), 0, ROWS - 1).astype(jnp.int32),
        "lengths": draw_lengths(jax.random.fold_in(key_list[12], 71), 0),
        "lhs_emb": bell_draw(key_list[6], (NPART, ROWS, D), 0.25, 1.5, ((0, 256),), jnp.float32),
        "lhs_acc": jnp.clip(jnp.exp(math.log(1.0) - 4.6051702 * jax.random.uniform(key_list[7], (NPART, ROWS), jnp.float32) ** block_scale(key_list[7], (NPART, ROWS), ((0, 256),), -0.2, 0.2)), 0.01, 1.0),
        "rhs_emb": bell_draw(key_list[8], (NPART, ROWS, D), 0.25, 1.5, ((0, 256),), jnp.float32),
        "rhs_acc": jnp.clip(jnp.exp(math.log(1.0) - 4.6051702 * jax.random.uniform(key_list[9], (NPART, ROWS), jnp.float32) ** block_scale(key_list[9], (NPART, ROWS), ((0, 256),), -0.2, 0.2)), 0.01, 1.0),
        "relation": jnp.clip(1.0 + 0.18 * jax.random.normal(key_list[10], (NREL, D), jnp.float32), 0.1, 1.9),
        "rel_acc": jnp.clip(jnp.exp(jax.random.uniform(key_list[11], (NREL,), jnp.float32, math.log(0.01), math.log(1.0))), 0.01, 1.0),
    }


LEARN_RATE = 0.1
EXACT = lax.Precision.HIGHEST

def adagrad_rows(embedded, totals, gradient):
    totals = totals + lax.optimization_barrier(jnp.mean(gradient * gradient, axis=1))
    return (embedded - LEARN_RATE * gradient / jnp.sqrt(totals)[:, None], totals)

def train_bucket(source_block, source_totals, target_block, target_totals, relation, lhs_rows, rhs_rows, type_rows, negative_rows, filled):
    neg_scale = 1.0 / math.sqrt(NNEG)

    def one_batch(state_now, inputs):
        source_block, source_totals, target_block, target_totals, relation_grad = state_now
        lhs_index, rhs_index, type_index, negative_index, length_now = inputs
        live_mask = (jnp.arange(BATCH, dtype=jnp.int32) < length_now).astype(jnp.float32)
        operator = relation[type_index]
        source_rows = source_block[lhs_index]
        target_rows = target_block[rhs_index]
        negative_emb = target_block[negative_index]
        product = source_rows * operator
        positive = lax.optimization_barrier(jnp.sum(product * target_rows, axis=1))
        negative = lax.dot_general(product, negative_emb, (((1,), (1,)), ((), ())), precision=EXACT)
        pos_weight = (jax.nn.sigmoid(positive) - 1.0) * live_mask
        neg_weight = jax.nn.sigmoid(negative) * (live_mask * neg_scale)[:, None]
        backward = pos_weight[:, None] * target_rows + jnp.dot(neg_weight, negative_emb, precision=EXACT)
        source_grad = jnp.zeros_like(source_block).at[lhs_index].add(backward * operator)
        negative_grad = lax.dot_general(neg_weight, product, (((0,), (0,)), ((), ())), precision=EXACT)
        target_grad = jnp.zeros_like(target_block).at[rhs_index].add(pos_weight[:, None] * product)
        target_grad = target_grad.at[negative_index].add(negative_grad)
        relation_grad = relation_grad + jax.ops.segment_sum(backward * source_rows, type_index, num_segments=NREL)
        source_block, source_totals = adagrad_rows(source_block, source_totals, source_grad)
        target_block, target_totals = adagrad_rows(target_block, target_totals, target_grad)
        return ((source_block, source_totals, target_block, target_totals, relation_grad), None)
    initial = (source_block, source_totals, target_block, target_totals, jnp.zeros_like(relation))
    finished, _ = lax.scan(one_batch, initial, (lhs_rows, rhs_rows, type_rows, negative_rows, filled))
    return finished

def per_bucket(values, round_no):
    picked = values[round_no]
    return picked.reshape((NPART, BATCHES) + picked.shape[1:])

def reference(plan, lhs_ids, rhs_ids, rel_ids, neg_ids, lengths, lhs_emb, lhs_acc, rhs_emb, rhs_acc, relation, rel_acc):
    device_no = jnp.arange(NPART, dtype=jnp.int32)
    source_coord = device_no // N_DST
    target_coord = device_no % N_DST
    relation_sum = jnp.zeros_like(relation)
    for round_no in range(ROUNDS):
        src_offset = plan[round_no, 0]
        dst_offset = plan[round_no, 1]
        source_part = (jnp.bitwise_xor(source_coord, src_offset) * N_DST + target_coord).astype(jnp.int32)
        target_part = (source_coord * N_DST + jnp.bitwise_xor(target_coord, dst_offset)).astype(jnp.int32)
        trained = jax.vmap(train_bucket, in_axes=(0, 0, 0, 0, None, 0, 0, 0, 0, 0))(lhs_emb[source_part], lhs_acc[source_part], rhs_emb[target_part], rhs_acc[target_part], relation, per_bucket(lhs_ids, round_no), per_bucket(rhs_ids, round_no), per_bucket(rel_ids, round_no), per_bucket(neg_ids, round_no), per_bucket(lengths, round_no))
        lhs_emb = lhs_emb.at[source_part].set(trained[0])
        lhs_acc = lhs_acc.at[source_part].set(trained[1])
        rhs_emb = rhs_emb.at[target_part].set(trained[2])
        rhs_acc = rhs_acc.at[target_part].set(trained[3])
        relation_sum = relation_sum + lax.optimization_barrier(jnp.sum(trained[4], axis=0))
    rel_acc_out = rel_acc + lax.optimization_barrier(jnp.mean(relation_sum * relation_sum, axis=1))
    relation_out = relation - LEARN_RATE * relation_sum / jnp.sqrt(rel_acc_out)[:, None]
    return (lhs_emb, lhs_acc, rhs_emb, rhs_acc, relation_out, rel_acc_out)
```

```python
import functools
import math

import jax
import jax.numpy as jnp
from jax import lax
from jax.experimental import pallas as pl
from jax.experimental.pallas import tpu as pltpu
from jax.sharding import PartitionSpec as P

LEARN_RATE = 0.1
F32 = jnp.float32
BF16 = jnp.bfloat16


def halves(values):
    high = values.astype(BF16)
    return high, (values - high.astype(F32)).astype(BF16)


def nn(a, b):
    return jnp.dot(a, b, preferred_element_type=F32)


def nt(a, b):
    return lax.dot_general(a, b, (((1,), (1,)), ((), ())), preferred_element_type=F32)


def three(product, a, b):
    return product(a[0], b[0]) + (product(a[0], b[1]) + product(a[1], b[0]))


def hits(ids, count):
    rows = lax.broadcasted_iota(jnp.int32, (count, ids.shape[1]), 0)
    return rows == ids


def train_kernel(live_ref, len_ref, lhs_ref, rhs_ref, rel_ref, neg_ref, left_ref, right_ref, relation_ref,
                 left_out, right_out, grad_out, left, right, left_acc, right_acc, grad, operators):
    rows = left.shape[1]
    width = left.shape[0]
    types = relation_ref.shape[0]
    wide = 2 * types
    batch = lhs_ref.shape[1]
    scale = 1.0 / math.sqrt(neg_ref.shape[1])
    rest = rows - width
    for source, block, totals in ((left_ref, left, left_acc), (right_ref, right, right_acc)):
        block[...] = source[0:rows, :].T
        totals[0:1, 0:width] = source[rows : rows + 1, :]
        totals[0:1, width:rows] = source[rows + 1 : rows + 2, 0:rest]
    rel_high, rel_low = halves(relation_ref[...])
    operators[...] = jnp.concatenate([rel_high.astype(F32), rel_low.astype(F32)], axis=0).T.astype(BF16)
    grad[...] = jnp.zeros_like(grad)

    def adagrad(block, totals, gradient):
        total = totals[0:1, :] + jnp.sum(gradient * gradient, axis=0, keepdims=True) * (1.0 / width)
        totals[0:1, :] = total
        block[...] = block[...] - gradient * (LEARN_RATE * lax.rsqrt(total))

    def one_batch(number, carry):
        pick = pl.ds(number, 1)
        lhs_hit = hits(lhs_ref[pick, :], rows).astype(F32).astype(BF16)
        rhs_hit = hits(rhs_ref[pick, :], rows)
        rel_hit = hits(rel_ref[pick, :], wide).astype(F32).astype(BF16)
        rel_both = hits(rel_ref[pick, :], types).astype(F32).astype(BF16)
        neg_hit = hits(neg_ref[pick, :], rows).astype(F32).astype(BF16)
        live = lax.broadcasted_iota(jnp.int32, (1, batch), 1) < len_ref[number]
        times = nn(neg_hit, jnp.full((batch, 128), scale, BF16))
        times = jnp.concatenate([times] * (batch // 128), axis=1)
        left_high, left_low = halves(left[...])
        right_halves = halves(right[...])
        tall = right[...].T
        source_rows = nn(left_high, lhs_hit) + nn(left_low, lhs_hit)
        operator = nn(operators[...], jnp.concatenate([rel_both, rel_both], axis=0))
        product = source_rows * operator
        product_halves = halves(product)
        score = three(nn, halves(tall), product_halves)
        sigmoid = 0.5 * jnp.tanh(0.5 * score) + 0.5
        positive = rhs_hit.astype(F32)
        weight = sigmoid * (times + positive) - positive
        weight = jnp.where(live, weight, 0.0)
        weight_halves = halves(weight)
        backward = three(nn, right_halves, weight_halves)
        right_grad = three(nt, product_halves, weight_halves)
        adagrad(right, right_acc, right_grad)
        back_high, back_low = halves(backward * operator)
        left_grad = nt(back_high, lhs_hit) + nt(back_low, lhs_hit)
        adagrad(left, left_acc, left_grad)
        own_high, own_low = halves(backward * source_rows)
        grad[...] += nt(own_high, rel_hit) + nt(own_low, rel_hit)
        return carry

    lax.fori_loop(0, live_ref[0], one_batch, 0)
    for out, block, totals in ((left_out, left, left_acc), (right_out, right, right_acc)):
        out[0:rows, :] = block[...].T
        out[rows : rows + 8, :] = jnp.zeros((8, width), F32)
        out[rows : rows + 1, :] = totals[0:1, 0:width]
        out[rows + 1 : rows + 2, 0:rest] = totals[0:1, width:rows]
    grad_out[...] = grad[...].T[0:types, :]


def train(left, right, relation, lhs_ids, rhs_ids, rel_ids, neg_ids, lengths):
    packed, width = left.shape
    rows = packed - 8
    types = relation.shape[0]
    live = jnp.sum((lengths > 0).astype(jnp.int32)).reshape(1)
    smem = pl.BlockSpec(memory_space=pltpu.SMEM)
    vmem = pl.BlockSpec(memory_space=pltpu.VMEM)
    block = jax.ShapeDtypeStruct((packed, width), F32)
    return pl.pallas_call(
        train_kernel,
        out_shape=(block, block, jax.ShapeDtypeStruct((types, width), F32)),
        in_specs=[smem, smem] + [vmem] * 7,
        out_specs=(vmem, vmem, vmem),
        scratch_shapes=[
            pltpu.VMEM((width, rows), F32),
            pltpu.VMEM((width, rows), F32),
            pltpu.VMEM((8, rows), F32),
            pltpu.VMEM((8, rows), F32),
            pltpu.VMEM((width, 2 * types), F32),
            pltpu.VMEM((width, 2 * types), BF16),
        ],
        compiler_params=pltpu.CompilerParams(vmem_limit_bytes=40 * 1024 * 1024),
    )(live, lengths, lhs_ids, rhs_ids, rel_ids, neg_ids, left, right, relation)


def pack(block, totals):
    rows, width = block.shape
    flat = jnp.concatenate([totals, jnp.zeros((8 * width - rows,), F32)])
    return jnp.concatenate([block, flat.reshape(8, width)], axis=0)


def unpack(packed):
    rows = packed.shape[0] - 8
    return packed[:rows], packed[rows:].reshape(-1)[:rows]


def flips(count, offset):
    return [(index, index ^ offset) for index in range(count)]


def exchange(block, axis, offset):
    return lax.ppermute(block, axis, flips(lax.axis_size(axis), offset))


def moved(block, axis, offset):
    count = lax.axis_size(axis)
    routes = [functools.partial(exchange, axis=axis, offset=step) for step in range(1, count)]
    return lax.switch(offset - 1, routes, block)


def levels(axis, first=0):
    return [(axis, 1 << bit) for bit in range(first, lax.axis_size(axis).bit_length() - 1)]


def added(gradient, steps):
    for axis, step in steps:
        gradient = gradient + exchange(gradient, axis, step)
    return gradient


def deep_route(block, gradient, offset):
    block = exchange(block, "dst", offset) if offset else block
    return block, added(gradient, levels("dst", 1))


def on_device(plan, lhs_ids, rhs_ids, rel_ids, neg_ids, lengths, lhs_emb, lhs_acc, rhs_emb, rhs_acc, relation, rel_acc):
    left = pack(lhs_emb[0], lhs_acc[0])
    right = pack(rhs_emb[0], rhs_acc[0])
    left_at, right_at = jnp.int32(0), jnp.int32(0)
    gradient = jnp.zeros(relation.shape, F32)
    for turn in range(plan.shape[0]):
        left = moved(left, "src", left_at ^ plan[turn, 0])
        right = moved(right, "dst", right_at ^ plan[turn, 1])
        left_at, right_at = plan[turn, 0], plan[turn, 1]
        left, right, part = train(
            left, right, relation, lhs_ids[turn], rhs_ids[turn], rel_ids[turn], neg_ids[turn], lengths[turn]
        )
        gradient = gradient + part
    left = moved(left, "src", left_at)
    near = exchange(right, "dst", 1)
    right = jnp.where((right_at & 1) == 1, near, right)
    gradient = added(gradient, levels("src") + [("dst", 1)])
    half = lax.axis_size("dst") // 2
    routes = [functools.partial(deep_route, offset=2 * step) for step in range(half)]
    right, gradient = lax.switch(right_at >> 1, routes, right, gradient)
    left, left_acc = unpack(left)
    right, right_acc = unpack(right)
    rel_acc_out = rel_acc + jnp.mean(gradient * gradient, axis=1)
    relation_out = relation - LEARN_RATE * gradient / jnp.sqrt(rel_acc_out)[:, None]
    return left[None], left_acc[None], right[None], right_acc[None], relation_out, rel_acc_out


def solution(mesh):
    both = ("src", "dst")
    ids = P(None, both, None)
    blocks = (P(both, None, None), P(both, None)) * 2
    return jax.shard_map(
        on_device,
        mesh=mesh,
        in_specs=(P(), ids, ids, ids, ids, P(None, both)) + blocks + (P(), P()),
        out_specs=blocks + (P(), P()),
        check_vma=False,
    )
```

```python
import functools
import math

import jax
import jax.numpy as jnp
from jax import lax
from jax.experimental import pallas as pl
from jax.experimental.pallas import tpu as pltpu
from jax.sharding import PartitionSpec as P

LEARN_RATE = 0.1
F32 = jnp.float32
BF16 = jnp.bfloat16


def halves(values):
    high = values.astype(BF16)
    return high, (values - high.astype(F32)).astype(BF16)


def nn(a, b):
    return jnp.dot(a, b, preferred_element_type=F32)


def nt(a, b):
    return lax.dot_general(a, b, (((1,), (1,)), ((), ())), preferred_element_type=F32)


def three(product, a, b):
    return product(a[0], b[0]) + (product(a[0], b[1]) + product(a[1], b[0]))


def hits(ids, count):
    rows = lax.broadcasted_iota(jnp.int32, (count, ids.shape[1]), 0)
    return rows == ids


def train_kernel(turn_ref, len_ref, lhs_ref, rhs_ref, rel_ref, neg_ref, left_ref, right_ref, relation_ref, prior_ref,
                 left_out, right_out, grad_out, grad, operators):
    width = relation_ref.shape[1]
    rows = left_ref.shape[1]
    types = relation_ref.shape[0]
    wide = 2 * types
    turn = turn_ref[0]
    batches, batch = lhs_ref.shape[1:]
    scale = 1.0 / math.sqrt(neg_ref.shape[2])
    rel_high, rel_low = halves(relation_ref[...])
    operators[...] = jnp.concatenate([rel_high.astype(F32), rel_low.astype(F32)], axis=0).T.astype(BF16)
    grad[...] = jnp.zeros_like(grad)
    left_out[...] = left_ref[...]
    right_out[...] = right_ref[...]
    left, left_acc = left_out.at[0:width], left_out.at[width : width + 8]
    right, right_acc = right_out.at[0:width], right_out.at[width : width + 8]
    live_batches = jnp.int32(0)
    for number in range(batches):
        live_batches += (len_ref[turn, number] > 0).astype(jnp.int32)

    def adagrad(block, totals, gradient):
        total = totals[0:1, :] + jnp.sum(gradient * gradient, axis=0, keepdims=True) * (1.0 / width)
        totals[0:1, :] = total
        block[...] = block[...] - gradient * (LEARN_RATE * lax.rsqrt(total))

    def one_batch(number, carry):
        pick = pl.ds(number, 1)
        lhs_hit = hits(lhs_ref[turn, pick, :], rows).astype(F32).astype(BF16)
        rhs_hit = hits(rhs_ref[turn, pick, :], rows)
        rel_hit = hits(rel_ref[turn, pick, :], wide).astype(F32).astype(BF16)
        rel_both = hits(rel_ref[turn, pick, :], types).astype(F32).astype(BF16)
        neg_hit = hits(neg_ref[turn, pick, :], rows).astype(F32).astype(BF16)
        live = lax.broadcasted_iota(jnp.int32, (1, batch), 1) < len_ref[turn, number]
        times = nn(neg_hit, jnp.full((batch, 128), scale, BF16))
        times = jnp.concatenate([times] * (batch // 128), axis=1)
        left_high, left_low = halves(left[...])
        right_halves = halves(right[...])
        tall = right[...].T
        source_rows = nn(left_high, lhs_hit) + nn(left_low, lhs_hit)
        operator = nn(operators[...], jnp.concatenate([rel_both, rel_both], axis=0))
        product = source_rows * operator
        product_halves = halves(product)
        score = three(nn, halves(tall), product_halves)
        sigmoid = 0.5 * jnp.tanh(0.5 * score) + 0.5
        positive = rhs_hit.astype(F32)
        weight = sigmoid * (times + positive) - positive
        weight = jnp.where(live, weight, 0.0)
        weight_halves = halves(weight)
        backward = three(nn, right_halves, weight_halves)
        right_grad = three(nt, product_halves, weight_halves)
        adagrad(right, right_acc, right_grad)
        back_high, back_low = halves(backward * operator)
        left_grad = nt(back_high, lhs_hit) + nt(back_low, lhs_hit)
        adagrad(left, left_acc, left_grad)
        own_high, own_low = halves(backward * source_rows)
        grad[...] += nt(own_high, rel_hit) + nt(own_low, rel_hit)
        return carry

    lax.fori_loop(0, live_batches, one_batch, 0)
    grad_out[...] = prior_ref[...] + grad[...].T[0:types, :]


def train(turn, left, right, relation, prior, lengths, *ids):
    types, width = relation.shape
    smem = pl.BlockSpec(memory_space=pltpu.SMEM)
    vmem = pl.BlockSpec(memory_space=pltpu.VMEM)
    block = jax.ShapeDtypeStruct(left.shape, F32)
    return pl.pallas_call(
        train_kernel,
        out_shape=(block, block, jax.ShapeDtypeStruct((types, width), F32)),
        in_specs=[smem, smem] + [vmem] * 8,
        out_specs=(vmem, vmem, vmem),
        scratch_shapes=[pltpu.VMEM((width, 2 * types), F32), pltpu.VMEM((width, 2 * types), BF16)],
        compiler_params=pltpu.CompilerParams(vmem_limit_bytes=40 * 1024 * 1024),
    )(turn.reshape(1), lengths, *ids, left, right, relation, prior)


def pack_kernel(left_emb, left_acc, right_emb, right_acc, left_out, right_out):
    for block, totals, out in ((left_emb, left_acc, left_out), (right_emb, right_acc, right_out)):
        width = block.shape[2]
        out[0:width, :] = block[0].T
        out[width : width + 8, :] = jnp.broadcast_to(totals[...], (8, totals.shape[1]))


def pack(left_emb, left_acc, right_emb, right_acc):
    rows, width = left_emb.shape[1:]
    block = jax.ShapeDtypeStruct((width + 8, rows), F32)
    return pl.pallas_call(pack_kernel, out_shape=(block, block))(left_emb, left_acc, right_emb, right_acc)


def finish_kernel(plan, left, right, near, grad, relation, rel_acc, left_emb, left_acc, right_emb, right_acc, relation_out, acc_out):
    width = left_emb.shape[2]
    swapped = (plan[plan.shape[0] - 1, 1] & 1) == 1
    right_now = jnp.where(swapped, near[...], right[...])
    for block, emb, totals in ((left[...], left_emb, left_acc), (right_now, right_emb, right_acc)):
        emb[0] = block[0:width, :].T
        totals[...] = block[width : width + 1, :]
    types = relation.shape[0]
    gradient = grad[...]
    mean = jnp.sum(gradient * gradient, axis=1, keepdims=True) * (1.0 / width)
    across = lax.broadcasted_iota(jnp.int32, (types, types), 1)
    down = lax.broadcasted_iota(jnp.int32, (types, types), 0)
    before = jnp.broadcast_to(rel_acc[...], (types, types))
    total = mean + jnp.sum(jnp.where(across == down, before, 0.0), axis=1, keepdims=True)
    relation_out[...] = relation[...] - LEARN_RATE * gradient / jnp.sqrt(total)
    acc_out[...] = jnp.sum(jnp.where(across == down, total, 0.0), axis=0, keepdims=True)


def finish(plan, left, right, near, grad, relation, rel_acc):
    rows = left.shape[1]
    types, width = relation.shape
    shapes = [(1, rows, width), (1, rows)] * 2 + [(types, width), (1, types)]
    outs = pl.pallas_call(
        finish_kernel,
        in_specs=[pl.BlockSpec(memory_space=pltpu.SMEM)] + [pl.BlockSpec(memory_space=pltpu.VMEM)] * 6,
        out_shape=[jax.ShapeDtypeStruct(s, F32) for s in shapes],
    )(plan, left, right, near, grad, relation, rel_acc.reshape(1, types))
    return (*outs[:5], outs[5].reshape(types))


def flips(count, offset):
    return [(index, index ^ offset) for index in range(count)]


def exchange(block, axis, offset):
    return lax.ppermute(block, axis, flips(lax.axis_size(axis), offset))


def levels(axis, *bits):
    return [(axis, 1 << bit) for bit in bits]


def added(gradient, steps):
    for axis, step in steps:
        gradient = gradient + exchange(gradient, axis, step)
    return gradient


def route(block, gradient, axis, offset, steps):
    return exchange(block, axis, offset) if offset else block, added(gradient, steps)


def moved(block, axis, offset, gradient=(), steps=(), shift=0):
    offsets = range(0, lax.axis_size(axis), 1 << shift)
    routes = [functools.partial(route, axis=axis, offset=step, steps=steps) for step in offsets]
    return lax.switch(offset >> shift if shift else offset, routes, block, gradient)


def on_device(plan, lhs_ids, rhs_ids, rel_ids, neg_ids, lengths, lhs_emb, lhs_acc, rhs_emb, rhs_acc, relation, rel_acc):
    left, right = pack(lhs_emb, lhs_acc, rhs_emb, rhs_acc)
    gradient = jnp.zeros(relation.shape, F32)
    steps = jnp.concatenate([plan[:1], plan[1:] ^ plan[:-1]])

    def one_turn(turn, held):
        left, right, gradient = held
        left, _ = moved(left, "src", steps[turn, 0])
        right, _ = moved(right, "dst", steps[turn, 1])
        return train(turn, left, right, relation, gradient, lengths, lhs_ids, rhs_ids, rel_ids, neg_ids)

    left, right, gradient = lax.fori_loop(0, plan.shape[0], one_turn, (left, right, gradient))
    left_at, right_at = plan[-1, 0], plan[-1, 1]
    right, gradient = moved(right, "dst", right_at, gradient, levels("src", 2, 3) + levels("dst", 0), 1)
    left, _ = moved(left, "src", left_at)
    near = exchange(right, "dst", 1)
    gradient = added(gradient, levels("src", 0, 1) + levels("dst", 1, 2, 3))
    return finish(plan, left, right, near, gradient, relation, rel_acc)


def solution(mesh):
    both = ("src", "dst")
    ids = P(None, both, None)
    blocks = (P(both, None, None), P(both, None)) * 2
    return jax.shard_map(
        on_device,
        mesh=mesh,
        in_specs=(P(), ids, ids, ids, ids, P(None, both)) + blocks + (P(), P()),
        out_specs=blocks + (P(), P()),
        check_vma=False,
    )
```

```python
import functools
import math

import jax
import jax.numpy as jnp
from jax import lax
from jax.experimental import pallas as pl
from jax.experimental.pallas import tpu as pltpu
from jax.sharding import PartitionSpec as P

LEARN_RATE = 0.1
F32 = jnp.float32
BF16 = jnp.bfloat16


def halves(values):
    high = values.astype(BF16)
    return high, (values - high.astype(F32)).astype(BF16)


def nn(a, b):
    return jnp.dot(a, b, preferred_element_type=F32)


def nt(a, b):
    return lax.dot_general(a, b, (((1,), (1,)), ((), ())), preferred_element_type=F32)


def three(product, a, b):
    axis = 0 if product is nn else 1
    return product(jnp.concatenate([a[0], a[0], a[1]], axis=1), jnp.concatenate([b[0], b[1], b[0]], axis=axis))


def hits(ids, count):
    rows = lax.broadcasted_iota(jnp.int32, (count, ids.shape[1]), 0)
    return rows == ids


def train_kernel(turn_ref, len_ref, lhs_ref, rhs_ref, rel_ref, neg_ref, left_ref, right_ref, relation_ref, prior_ref,
                 left_out, right_out, grad_out, grad, operators):
    width = relation_ref.shape[1]
    rows = left_ref.shape[1]
    types = relation_ref.shape[0]
    wide = 2 * types
    turn = turn_ref[0]
    batches, batch = lhs_ref.shape[1:]
    scale = 1.0 / math.sqrt(neg_ref.shape[2])
    rel_high, rel_low = halves(relation_ref[...])
    operators[...] = jnp.concatenate([rel_high.astype(F32), rel_low.astype(F32)], axis=0).T.astype(BF16)
    grad[...] = jnp.zeros_like(grad)
    left_out[...] = left_ref[...]
    right_out[...] = right_ref[...]
    left, left_acc = left_out.at[0:width], left_out.at[width : width + 8]
    right, right_acc = right_out.at[0:width], right_out.at[width : width + 8]
    live_batches = jnp.int32(0)
    for number in range(batches):
        live_batches += (len_ref[turn, number] > 0).astype(jnp.int32)

    def adagrad(block, totals, gradient):
        total = totals[0:1, :] + jnp.sum(gradient * gradient, axis=0, keepdims=True) * (1.0 / width)
        totals[0:1, :] = total
        block[...] = block[...] - gradient * (LEARN_RATE * lax.rsqrt(total))

    def one_batch(number, carry):
        pick = pl.ds(number, 1)
        lhs_hit = hits(lhs_ref[turn, pick, :], rows).astype(F32).astype(BF16)
        rhs_hit = hits(rhs_ref[turn, pick, :], rows)
        rel_hit = hits(rel_ref[turn, pick, :], wide).astype(F32).astype(BF16)
        rel_both = hits(rel_ref[turn, pick, :], types).astype(F32).astype(BF16)
        neg_hit = hits(neg_ref[turn, pick, :], rows).astype(F32).astype(BF16)
        live = lax.broadcasted_iota(jnp.int32, (1, batch), 1) < len_ref[turn, number]
        times = nn(neg_hit, jnp.full((batch, 128), scale, BF16))
        times = jnp.concatenate([times] * (batch // 128), axis=1)
        left_high, left_low = halves(left[...])
        right_halves = halves(right[...])
        tall = right[...].T
        source_rows = nn(jnp.concatenate([left_high, left_low], axis=1), jnp.concatenate([lhs_hit, lhs_hit], axis=0))
        operator = nn(operators[...], jnp.concatenate([rel_both, rel_both], axis=0))
        product = source_rows * operator
        product_halves = halves(product)
        score = three(nn, halves(tall), product_halves)
        sigmoid = 0.5 * jnp.tanh(0.5 * score) + 0.5
        positive = rhs_hit.astype(F32)
        weight = sigmoid * (times + positive) - positive
        weight = jnp.where(live, weight, 0.0)
        weight_halves = halves(weight)
        backward = three(nn, right_halves, weight_halves)
        right_grad = three(nt, product_halves, weight_halves)
        adagrad(right, right_acc, right_grad)
        back_high, back_low = halves(backward * operator)
        left_grad = nt(jnp.concatenate([back_high, back_low], axis=1), jnp.concatenate([lhs_hit, lhs_hit], axis=1))
        adagrad(left, left_acc, left_grad)
        own_high, own_low = halves(backward * source_rows)
        grad[...] += nt(jnp.concatenate([own_high, own_low], axis=1), jnp.concatenate([rel_hit, rel_hit], axis=1))
        return carry

    lax.fori_loop(0, live_batches, one_batch, 0)
    grad_out[...] = prior_ref[...] + grad[...].T[0:types, :]


def train(turn, left, right, relation, prior, lengths, *ids):
    types, width = relation.shape
    smem = pl.BlockSpec(memory_space=pltpu.SMEM)
    vmem = pl.BlockSpec(memory_space=pltpu.VMEM)
    block = jax.ShapeDtypeStruct(left.shape, F32)
    return pl.pallas_call(
        train_kernel,
        out_shape=(block, block, jax.ShapeDtypeStruct((types, width), F32)),
        in_specs=[smem, smem] + [vmem] * 8,
        out_specs=(vmem, vmem, vmem),
        scratch_shapes=[pltpu.VMEM((width, 2 * types), F32), pltpu.VMEM((width, 2 * types), BF16)],
        compiler_params=pltpu.CompilerParams(vmem_limit_bytes=40 * 1024 * 1024),
    )(turn.reshape(1), lengths, *ids, left, right, relation, prior)


def pack_kernel(left_emb, left_acc, right_emb, right_acc, left_out, right_out):
    for block, totals, out in ((left_emb, left_acc, left_out), (right_emb, right_acc, right_out)):
        width = block.shape[2]
        out[0:width, :] = block[0].T
        out[width : width + 8, :] = jnp.broadcast_to(totals[...], (8, totals.shape[1]))


def pack(left_emb, left_acc, right_emb, right_acc):
    rows, width = left_emb.shape[1:]
    block = jax.ShapeDtypeStruct((width + 8, rows), F32)
    return pl.pallas_call(pack_kernel, out_shape=(block, block))(left_emb, left_acc, right_emb, right_acc)


def finish_kernel(plan, left, right, near, grad, relation, rel_acc, left_emb, left_acc, right_emb, right_acc, relation_out, acc_out):
    width = left_emb.shape[2]
    swapped = (plan[plan.shape[0] - 1, 1] & 1) == 1
    right_now = jnp.where(swapped, near[...], right[...])
    for block, emb, totals in ((left[...], left_emb, left_acc), (right_now, right_emb, right_acc)):
        emb[0] = block[0:width, :].T
        totals[...] = block[width : width + 1, :]
    types = relation.shape[0]
    gradient = grad[...]
    mean = jnp.sum(gradient * gradient, axis=1, keepdims=True) * (1.0 / width)
    across = lax.broadcasted_iota(jnp.int32, (types, types), 1)
    down = lax.broadcasted_iota(jnp.int32, (types, types), 0)
    before = jnp.broadcast_to(rel_acc[...], (types, types))
    total = mean + jnp.sum(jnp.where(across == down, before, 0.0), axis=1, keepdims=True)
    relation_out[...] = relation[...] - LEARN_RATE * gradient / jnp.sqrt(total)
    acc_out[...] = jnp.sum(jnp.where(across == down, total, 0.0), axis=0, keepdims=True)


def finish(plan, left, right, near, grad, relation, rel_acc):
    rows = left.shape[1]
    types, width = relation.shape
    shapes = [(1, rows, width), (1, rows)] * 2 + [(types, width), (1, types)]
    outs = pl.pallas_call(
        finish_kernel,
        in_specs=[pl.BlockSpec(memory_space=pltpu.SMEM)] + [pl.BlockSpec(memory_space=pltpu.VMEM)] * 6,
        out_shape=[jax.ShapeDtypeStruct(s, F32) for s in shapes],
    )(plan, left, right, near, grad, relation, rel_acc.reshape(1, types))
    return (*outs[:5], outs[5].reshape(types))


def flips(count, offset):
    return [(index, index ^ offset) for index in range(count)]


def exchange(block, axis, offset):
    return lax.ppermute(block, axis, flips(lax.axis_size(axis), offset))


def levels(axis, *bits):
    return [(axis, 1 << bit) for bit in bits]


def added(gradient, steps):
    for axis, step in steps:
        gradient = gradient + exchange(gradient, axis, step)
    return gradient


def route(block, gradient, axis, offset, steps):
    return exchange(block, axis, offset) if offset else block, added(gradient, steps)


def moved(block, axis, offset, gradient=(), steps=(), shift=0):
    offsets = range(0, lax.axis_size(axis), 1 << shift)
    routes = [functools.partial(route, axis=axis, offset=step, steps=steps) for step in offsets]
    return lax.switch(offset >> shift if shift else offset, routes, block, gradient)


def on_device(plan, lhs_ids, rhs_ids, rel_ids, neg_ids, lengths, lhs_emb, lhs_acc, rhs_emb, rhs_acc, relation, rel_acc):
    left, right = pack(lhs_emb, lhs_acc, rhs_emb, rhs_acc)
    gradient = jnp.zeros(relation.shape, F32)
    steps = jnp.concatenate([plan[:1], plan[1:] ^ plan[:-1]])

    def one_turn(turn, held):
        left, right, gradient = held
        left, _ = moved(left, "src", steps[turn, 0])
        right, _ = moved(right, "dst", steps[turn, 1])
        return train(turn, left, right, relation, gradient, lengths, lhs_ids, rhs_ids, rel_ids, neg_ids)

    left, right, gradient = lax.fori_loop(0, plan.shape[0], one_turn, (left, right, gradient))
    left_at, right_at = plan[-1, 0], plan[-1, 1]
    right, gradient = moved(right, "dst", right_at, gradient, levels("src", 2) + levels("dst", 0), 1)
    left, _ = moved(left, "src", left_at)
    near = exchange(right, "dst", 1)
    gradient = added(gradient, levels("src", 0, 1, 3) + levels("dst", 1, 2, 3))
    return finish(plan, left, right, near, gradient, relation, rel_acc)


def solution(mesh):
    both = ("src", "dst")
    ids = P(None, both, None)
    blocks = (P(both, None, None), P(both, None)) * 2
    return jax.shard_map(
        on_device,
        mesh=mesh,
        in_specs=(P(), ids, ids, ids, ids, P(None, both)) + blocks + (P(), P()),
        out_specs=blocks + (P(), P()),
        check_vma=False,
    )
```
